512 devices in a mesh: section: 8 (over y, core), dp: 64 (over x, z).
Axes of the slice: x: 4, y: 4, z: 16, core: 2. Of those that a mesh axis runs over, the one named last changes fastest.
Arguments:
- update: bfloat16 [8, 128, 64, 5120], P('section', 'dp'), may hold values from -6 to 6
- outgrad: bfloat16 [8, 128, 64, 13824], P('section', 'dp'), may hold values from -6 to 6
- basis: bfloat16 [8, 5120, 128], P('section', 'dp'), may hold values from -0.078125 to 0.078125
- counts: int32 [64], replicated, may hold values from 1 to 4, as said below
Outputs:
- eigvals: float32 [8, 256, 128, 128], P('section', 'dp')
The draws below stay inside these ranges and needn't reach their ends.
Inputs may be any that keep to these rules, and one draw needn't show every extreme that they name: counts sum to 108; owner o holds the blocks offsets[o] to offsets[o] + counts[o] - 1 in order.
All inputs are finite; a program needn't handle non-finite values.
Results may differ from the reference program's by a relative error of at most 0.0025.
Values may be sent and summed in bfloat16 or wider, within the bound.
No kernel may reach another device: no remote copies, remote signals or barrier semaphores. Data moves between devices by JAX's collectives and lax.ppermute only.
A program may use at most 128 MiB of HBM per device.

```python
import jax
import jax.numpy as jnp
from jax import lax

D = 5120
FW = 13824
BLK = 128
EIG = 128
SEQ_LEN = 64
LAYERS = 8
SEQS = 128
NBLK = 108
CAP = 4
N_DP = 64


def draw_counts(key, part):
    key = jax.random.fold_in(key, 11)
    remaining = NBLK - N_DP
    rank_order = jnp.arange(N_DP, dtype=jnp.int32)
    extra_blocks = jnp.clip(remaining - rank_order * (CAP - 1), 0, CAP - 1)
    shuffle = jax.random.permutation(key, N_DP)
    return jnp.zeros((N_DP,), jnp.int32).at[shuffle].set(1 + extra_blocks).astype(jnp.int32)


def block_scale(rng, shape, cuts, least, high):
    def one(dim, shards_of):
        heights = jax.random.uniform(jax.random.fold_in(jax.random.fold_in(rng, 6), dim), (shards_of,), jnp.float32, least / len(cuts), high / len(cuts))
        return jnp.repeat(jnp.exp(heights), shape[dim] // shards_of).reshape((-1,) + (1,) * (len(shape) - dim - 1))

    factor_of = one(*cuts[0])
    for cut in cuts[1:]:
        factor_of = factor_of * one(*cut)
    return factor_of


def scatter_about(stream_key, extent, spread, reach, split=(), held_as=jnp.bfloat16):
    gain = block_scale(stream_key, extent, split, -0.22, 0.18) if split else 1.0
    drawn = jax.random.normal(stream_key, extent, jnp.float32) * spread * gain
    return jnp.minimum(jnp.maximum(drawn, -reach), reach).astype(held_as)


def setup_inputs(seed: int = 0) -> dict:
    key_list = jax.random.split(jax.random.key(seed), 5)
    return {
        "update": scatter_about(key_list[0], (LAYERS, SEQS, SEQ_LEN, D), 1.0, 6.0, ((0, 8), (1, 64))),
        "outgrad": scatter_about(key_list[1], (LAYERS, SEQS, SEQ_LEN, FW), 1.0, 6.0, ((0, 8), (1, 64))),
        "basis": scatter_about(key_list[2], (LAYERS, D, EIG), D ** -0.5, 0.078125, ((0, 8), (1, 64))),
        "counts": draw_counts(jax.random.fold_in(key_list[4], 71), 0),
    }


def reference(update, outgrad, basis, counts):
    prefix = jnp.cumsum(update.astype(jnp.float32), axis=0)
    mlp_in = prefix.astype(jnp.bfloat16)
    offsets = jnp.cumsum(counts) - counts
    slot_range = jnp.arange(CAP, dtype=jnp.int32)
    block_index = offsets[:, None] + slot_range[None, :]
    slot_valid = slot_range[None, :] < counts[:, None]
    block_index = jnp.minimum(block_index, NBLK - 1).reshape(-1)

    def one_layer(arrays):
        inputs, gradients, vectors = arrays
        rotated = jnp.einsum("ntd,de->nte", inputs.astype(jnp.float32), vectors.astype(jnp.float32)).astype(jnp.bfloat16)

        def accumulate(running, pair_items):
            grad_rows, rot_rows = pair_items
            project = jnp.dot(grad_rows.T, rot_rows, preferred_element_type=jnp.float32) / SEQ_LEN
            return running + project * project, None

        running, _ = lax.scan(accumulate, jnp.zeros((FW, EIG), jnp.float32), (gradients, rotated))
        eigen_table = (running / SEQS).reshape(NBLK, BLK, EIG)
        picked = eigen_table[block_index].reshape(N_DP, CAP, BLK, EIG)
        filled = jnp.where(slot_valid[:, :, None, None], picked, jnp.float32(0.0))
        return filled.reshape(N_DP * CAP, BLK, EIG)

    return lax.map(one_layer, (mlp_in, outgrad, basis))
```

```python
import jax
import jax.numpy as jnp
from jax import lax
from jax.experimental import pallas as pl
from jax.experimental.pallas import tpu as pltpu
from jax.sharding import Mesh
from jax.sharding import PartitionSpec as P

D = 5120
FW = 13824
BLK = 128
EIG = 128
SEQ_LEN = 64
SEQS = 128
NBLK = FW // BLK
CAP = 4
N_X = 4
N_Z = 16
TOK = 128
PLANE = D // N_X
PER = 7
WID = PER * BLK
N_NEAR = 4
GROUP = N_X * N_NEAR
SECTION = ("y", "c")
DP = ("x", "z")

SMEM = pl.BlockSpec(memory_space=pltpu.SMEM)
VMEM = pl.BlockSpec(memory_space=pltpu.VMEM)


def sds(shape, dtype):
    return jax.ShapeDtypeStruct(shape, dtype)


def mod(a, n):
    return lax.rem(a + 4 * n, n)


def rotate_kernel(place, mine, other, *refs):
    bases = refs[:N_X]
    out, full = refs[N_X:]
    x, core = place[0], place[2]
    full[core] = mine[...]
    full[1 - core] = other[...]
    total = jnp.zeros((TOK, EIG), jnp.float32)
    for dx in range(N_X):
        rows = mod(x - dx, N_X)
        lane = pl.multiple_of(lax.rem(rows, 2) * PLANE, 128)
        part = full[rows // 2, :, pl.ds(lane, PLANE)]
        total = total + jnp.dot(part, bases[dx][...], preferred_element_type=jnp.float32)
    out[...] = total.T.astype(jnp.bfloat16)


def rotate(place, mine, other, bases):
    return pl.pallas_call(
        rotate_kernel,
        out_shape=sds((EIG, TOK), jnp.bfloat16),
        in_specs=[SMEM] + [VMEM] * (2 + N_X),
        out_specs=VMEM,
        scratch_shapes=[pltpu.VMEM((2, TOK, D // 2), jnp.bfloat16)],
        compiler_params=pltpu.CompilerParams(vmem_limit_bytes=32 * 2**20),
        name="rotate",
    )(place, mine, other, *bases)


def deal_kernel(counts, outgrad, out, column_of, offsets, block_of):
    def prefix(o, run):
        offsets[o] = run
        return run + counts[o]

    lax.fori_loop(0, N_X * N_Z, prefix, jnp.int32(0))

    def fill(i, _):
        column_of[i] = N_Z
        block_of[i] = 0
        return 0

    lax.fori_loop(0, 128, fill, 0)

    def owner(i, g):
        column = i // N_X
        o = lax.rem(i, N_X) * N_Z + column

        def block(s, _):
            block_of[g + s] = offsets[o] + s
            column_of[g + s] = column
            return 0

        lax.fori_loop(0, counts[o], block, 0)
        return g + counts[o]

    lax.fori_loop(0, N_X * N_Z, owner, jnp.int32(0))
    for m in range(GROUP):
        plane, member = m // N_NEAR, m % N_NEAR
        for j in range(PER):
            lane = pl.multiple_of(block_of[16 * j + 4 * member + plane] * BLK, BLK)
            for n in range(2):
                rows = slice(n * SEQ_LEN, (n + 1) * SEQ_LEN)
                out[m, rows, j * BLK : (j + 1) * BLK] = outgrad[0, n, :, pl.ds(lane, BLK)]


def deal(counts, outgrad):
    return pl.pallas_call(
        deal_kernel,
        out_shape=[sds((GROUP, TOK, WID), jnp.bfloat16), sds((128,), jnp.int32)],
        in_specs=[SMEM, VMEM],
        out_specs=[VMEM, SMEM],
        scratch_shapes=[pltpu.SMEM((N_X * N_Z,), jnp.int32), pltpu.SMEM((128,), jnp.int32)],
        compiler_params=pltpu.CompilerParams(vmem_limit_bytes=32 * 2**20),
        name="deal_blocks",
    )(counts, outgrad)


def square_kernel(place, column_of, *refs):
    rots, grad = refs[:N_X], refs[N_X]
    out, lhs, acc = refs[N_X + 1 :]
    x, member = place[0], place[3]
    lane = lax.broadcasted_iota(jnp.int32, (EIG, TOK), 1)
    zero = jnp.zeros((EIG, TOK), jnp.bfloat16)
    for dx in range(N_X):
        for k in range(N_NEAR):
            m = N_NEAR * mod(x - dx, N_X) + mod(member - k, N_NEAR)
            rot = rots[dx][k]
            lhs[m, :EIG, :] = jnp.where(lane < SEQ_LEN, rot, zero)
            lhs[m, EIG:, :] = jnp.where(lane < SEQ_LEN, zero, rot)
    for lo in range(0, WID, 256):
        hi = min(lo + 256, WID)

        def step(i, run):
            made = jnp.dot(lhs[i], grad[i, :, lo:hi], preferred_element_type=jnp.float32)
            return run + (made[:EIG] * made[:EIG] + made[EIG:] * made[EIG:])

        acc[:, lo:hi] = lax.fori_loop(0, GROUP, step, jnp.zeros((EIG, hi - lo), jnp.float32), unroll=4)
    out[...] = jnp.zeros(out.shape, out.dtype)
    first = 4 * member + x
    for j in range(PER):
        column = column_of[16 * j + first]

        @pl.when(column < N_Z)
        def _():
            out[column] = acc[:, j * BLK : (j + 1) * BLK].astype(out.dtype)


def square(place, column_of, rots, grads):
    return pl.pallas_call(
        square_kernel,
        out_shape=sds((N_Z, EIG, BLK), jnp.bfloat16),
        in_specs=[SMEM, SMEM] + [VMEM] * (N_X + 1),
        out_specs=VMEM,
        scratch_shapes=[
            pltpu.VMEM((GROUP, 2 * EIG, TOK), jnp.bfloat16),
            pltpu.VMEM((EIG, WID), jnp.float32),
        ],
        compiler_params=pltpu.CompilerParams(vmem_limit_bytes=32 * 2**20),
        name="square_sums",
    )(place, column_of, *rots, grads)


def column_starts(counts, z):
    def add(o, run):
        return run + jnp.where(lax.rem(o, N_Z) < z, counts[o], 0)

    start = lax.fori_loop(0, N_X * N_Z, add, jnp.int32(0))
    starts = []
    for k in range(N_X):
        starts.append(start)
        start = start + counts[k * N_Z + z]
    return starts


def gather_kernel(place, counts, got, out):
    x, z, core = place[0], place[1], place[2]
    for k, start in enumerate(column_starts(counts, z)):
        g = start + mod(x - start + 128, N_X)
        member = lax.rem(g // 4 + 2 * core, N_NEAR)
        owned = g < start + counts[k * N_Z + z]

        @pl.when(owned)
        def _():
            total = got[member].astype(jnp.float32)
            for far in range(4, N_Z, 4):
                total = total + got[member + far].astype(jnp.float32)
            out[k] = total

        @pl.when(jnp.logical_not(owned))
        def _():
            out[k] = jnp.zeros((EIG, BLK), jnp.float32)


def gather_nodes(place, counts, got):
    return pl.pallas_call(
        gather_kernel,
        out_shape=sds((N_X, EIG, BLK), jnp.float32),
        in_specs=[SMEM, SMEM, VMEM],
        out_specs=VMEM,
        name="gather_nodes",
    )(place, counts, got)


def finish_kernel(place, counts, got, out):
    x, z = place[0], place[1]
    starts = column_starts(counts, z)
    start = jnp.int32(0)
    for k in range(N_X):
        start = start + jnp.where(x == k, starts[k], 0)
    owned = counts[x * N_Z + z]
    scale = 1.0 / (SEQ_LEN * SEQ_LEN * SEQS)
    for s in range(CAP):
        plane = lax.rem(start + s, N_X)
        out[0, s] = jnp.where(s < owned, got[plane].T * scale, 0.0)


def finish(place, counts, got):
    return pl.pallas_call(
        finish_kernel,
        out_shape=sds((1, CAP, BLK, EIG), jnp.float32),
        in_specs=[SMEM, SMEM, VMEM],
        out_specs=VMEM,
        name="finish",
    )(place, counts, got)


def group_line(core, start):
    return [(start + 2 * core + r) % N_Z for r in range(N_NEAR)]


def index(y, core, x, z):
    return ((2 * y + core) * N_X + x) * N_Z + z


def group_exchange(v):
    groups = [
        [index(y, c, x, z) for x in range(N_X) for z in group_line(c, start)]
        for y in range(4)
        for c in range(2)
        for start in range(0, N_Z, N_NEAR)
    ]
    return lax.all_to_all(v, SECTION + DP, 0, 0, axis_index_groups=groups, tiled=True)


def group_share(v):
    line = [v]
    for k in range(1, N_NEAR):
        perm = [
            (c * N_Z + zs[r], c * N_Z + zs[(r + k) % N_NEAR])
            for c in range(2)
            for start in range(0, N_Z, N_NEAR)
            for zs in [group_line(c, start)]
            for r in range(N_NEAR)
        ]
        line.append(lax.ppermute(v, ("c", "z"), perm))
    line = jnp.stack(line)
    return [shift(line, "x", dx) for dx in range(N_X)]


def shift(v, axis, k):
    n = lax.axis_size(axis)
    return v if k == 0 else lax.ppermute(v, axis, [(i, (i + k) % n) for i in range(n)])


def stream(update):
    core = lax.axis_index("c")
    own = update[0].reshape(TOK, D)
    mine = lax.dynamic_slice_in_dim(own, core * (D // 2), D // 2, 1)
    theirs = shift(lax.dynamic_slice_in_dim(own, (1 - core) * (D // 2), D // 2, 1), "c", 1)
    mine, theirs = mine.astype(jnp.float32), theirs.astype(jnp.float32)
    pair = (mine + theirs).astype(jnp.bfloat16)
    steps = [lax.ppermute(pair, "y", [(i, i + k) for i in range(4 - k)]) for k in range(1, 4)]
    before = steps[0].astype(jnp.float32) + steps[1].astype(jnp.float32) + steps[2].astype(jnp.float32)
    low = before + jnp.where(core == 0, mine, theirs)
    high = low + jnp.where(core == 0, theirs, mine)
    low, high = low.astype(jnp.bfloat16), high.astype(jnp.bfloat16)
    return jnp.where(core == 0, low, high), shift(jnp.where(core == 0, high, low), "c", 1)


def per_device(update, outgrad, basis, counts):
    x, z, core = lax.axis_index("x"), lax.axis_index("z"), lax.axis_index("c")
    place = jnp.stack([x, z, core, (z + 2 * core) % N_NEAR]).astype(jnp.int32)
    dealt, column_of = deal(counts, outgrad)
    line = lax.all_to_all(jnp.broadcast_to(basis, (N_Z,) + basis.shape[1:]), "z", 0, 0, tiled=True)
    line, dealt = lax.optimization_barrier((line.reshape(PLANE, EIG), dealt))
    grads = group_exchange(dealt)
    bases = [shift(line, "x", dx) for dx in range(N_X)]
    mine, other = stream(update)
    rots = group_share(rotate(place, mine, other, bases))
    got = lax.all_to_all(square(place, column_of, rots, grads), "z", 0, 0, tiled=True)
    got = lax.all_to_all(gather_nodes(place, counts, got), "x", 0, 0, tiled=True)
    return finish(place, counts, got)


def solution(mesh):
    fine = Mesh(mesh.devices.reshape(4, 2, N_X, N_Z), SECTION + DP)
    return jax.shard_map(
        per_device,
        mesh=fine,
        in_specs=(P(SECTION, DP, None, None), P(SECTION, DP, None, None), P(SECTION, DP, None), P()),
        out_specs=P(SECTION, DP, None, None),
        check_vma=False,
    )
```

```python
import jax
import jax.numpy as jnp
from jax import lax
from jax.experimental import pallas as pl
from jax.experimental.pallas import tpu as pltpu
from jax.sharding import Mesh
from jax.sharding import PartitionSpec as P

D = 5120
FW = 13824
BLK = 128
EIG = 128
SEQ_LEN = 64
SEQS = 128
NBLK = FW // BLK
CAP = 4
N_X = 4
N_Z = 16
TOK = 128
PLANE = D // N_X
SLOTS = 56
WID = SLOTS * BLK
PER = 7
GROUP = 8
SECTION = ("y", "c")
DP = ("x", "z")

SMEM = pl.BlockSpec(memory_space=pltpu.SMEM)
VMEM = pl.BlockSpec(memory_space=pltpu.VMEM)


def sds(shape, dtype):
    return jax.ShapeDtypeStruct(shape, dtype)


def mod(a, n):
    return lax.rem(a + 4 * n, n)


def rotate_kernel(place, mine, other, *refs):
    bases = refs[:N_X]
    out, full = refs[N_X:]
    x, core = place[0], place[2]
    full[core] = mine[...]
    full[1 - core] = other[...]
    total = jnp.zeros((TOK, EIG), jnp.float32)
    for dx in range(N_X):
        rows = mod(x - dx, N_X)
        lane = pl.multiple_of(lax.rem(rows, 2) * PLANE, 128)
        part = full[rows // 2, :, pl.ds(lane, PLANE)]
        total = total + jnp.dot(part, bases[dx][...], preferred_element_type=jnp.float32)
    out[...] = total.T.astype(jnp.bfloat16)


def rotate(place, mine, other, bases):
    return pl.pallas_call(
        rotate_kernel,
        out_shape=sds((EIG, TOK), jnp.bfloat16),
        in_specs=[SMEM] + [VMEM] * (2 + N_X),
        out_specs=VMEM,
        scratch_shapes=[pltpu.VMEM((2, TOK, D // 2), jnp.bfloat16)],
        compiler_params=pltpu.CompilerParams(vmem_limit_bytes=32 * 2**20),
        name="rotate",
    )(place, mine, other, *bases)


def deal_kernel(place, counts, outgrad, kept, sent_up, sent_down, column_of, starts, offsets, block_of):
    z = place[1]

    def prefix(o, run):
        offsets[o] = run
        return run + counts[o]

    lax.fori_loop(0, N_X * N_Z, prefix, jnp.int32(0))

    def fill(i, _):
        column_of[i] = N_Z
        block_of[i] = 0
        return 0

    lax.fori_loop(0, 128, fill, 0)

    def owner(i, g):
        column = i // N_X
        o = lax.rem(i, N_X) * N_Z + column

        @pl.when(column == z)
        def _():
            starts[lax.rem(i, N_X)] = g

        def block(s, _):
            block_of[g + s] = offsets[o] + s
            column_of[g + s] = column
            return 0

        lax.fori_loop(0, counts[o], block, 0)
        return g + counts[o]

    lax.fori_loop(0, N_X * N_Z, owner, jnp.int32(0))
    for m in range(2):
        near = lax.rem(place[3] + m, 2)
        for i in range(SLOTS):
            g = 16 * (i // 8) + 8 * (i // 4 % 2) + 4 * near + i % 4
            lane = pl.multiple_of(block_of[g] * BLK, BLK)
            for n in range(2):
                out = (kept.at[n * SEQ_LEN : (n + 1) * SEQ_LEN], (sent_up, sent_down)[n])[m]
                out[:, i * BLK : (i + 1) * BLK] = outgrad[0, n, :, pl.ds(lane, BLK)]


def deal(place, counts, outgrad):
    return pl.pallas_call(
        deal_kernel,
        out_shape=[sds((rows, WID), jnp.bfloat16) for rows in (TOK, SEQ_LEN, SEQ_LEN)] + [sds((128,), jnp.int32), sds((N_X,), jnp.int32)],
        in_specs=[SMEM, SMEM, VMEM],
        out_specs=[VMEM, VMEM, VMEM, SMEM, SMEM],
        scratch_shapes=[pltpu.SMEM((N_X * N_Z,), jnp.int32), pltpu.SMEM((128,), jnp.int32)],
        compiler_params=pltpu.CompilerParams(vmem_limit_bytes=32 * 2**20),
        name="deal_blocks",
    )(place, counts, outgrad)


def square_kernel(*refs):
    (own, up, down), (kept, got_up, got_down) = refs[:3], refs[3:6]
    out, lhs = refs[6:]
    lane = lax.broadcasted_iota(jnp.int32, (EIG, TOK), 1)
    zero = jnp.zeros((EIG, TOK), jnp.bfloat16)
    lhs[:EIG, :] = jnp.where(lane < SEQ_LEN, own[...], zero)
    lhs[EIG:, :] = jnp.where(lane < SEQ_LEN, zero, own[...])
    first, second = up[:, :SEQ_LEN], down[:, SEQ_LEN:]
    for i in range(0, SLOTS, 2):
        cols = slice(i * BLK, (i + 2) * BLK)
        made = jnp.dot(lhs[...], kept[:, cols], preferred_element_type=jnp.float32)
        made = made * made
        total = made[:EIG] + made[EIG:]
        for rot, grad in ((first, got_up), (second, got_down)):
            made = jnp.dot(rot, grad[:, cols], preferred_element_type=jnp.float32)
            total = total + made * made
        for k in range(2):
            member = 2 * ((i + k) % 4) + (i + k) // 4 % 2
            out[member, i // 8] = total[:, k * BLK : (k + 1) * BLK].astype(out.dtype)


def square(rots, grads):
    return pl.pallas_call(
        square_kernel,
        out_shape=sds((GROUP, PER, EIG, BLK), jnp.bfloat16),
        in_specs=[VMEM] * 6,
        out_specs=VMEM,
        scratch_shapes=[pltpu.VMEM((2 * EIG, TOK), jnp.bfloat16)],
        compiler_params=pltpu.CompilerParams(vmem_limit_bytes=32 * 2**20),
        name="square_sums",
    )(*rots, *grads)


def group_kernel(place, column_of, got, out):
    first = 4 * place[3] + place[0]
    out[...] = jnp.zeros(out.shape, out.dtype)
    for j in range(PER):
        column = column_of[16 * j + first]

        @pl.when(column < N_Z)
        def _():
            total = got[0, j].astype(jnp.float32)
            for r in range(1, GROUP):
                total = total + got[r, j].astype(jnp.float32)
            out[column] = total.astype(out.dtype)


def group_sums(place, column_of, got):
    return pl.pallas_call(
        group_kernel,
        out_shape=sds((N_Z, EIG, BLK), jnp.bfloat16),
        in_specs=[SMEM, SMEM, VMEM],
        out_specs=VMEM,
        name="group_sums",
    )(place, column_of, got)


def gather_kernel(place, counts, starts, got, out):
    x, z, core = place[0], place[1], place[2]
    for k in range(N_X):
        start = starts[k]
        g = start + mod(x - start + 128, N_X)
        member = lax.rem(g // 4 + 2 * core, 4)
        owned = g < start + counts[k * N_Z + z]

        @pl.when(owned)
        def _():
            total = got[member].astype(jnp.float32)
            for far in range(4, N_Z, 4):
                total = total + got[member + far].astype(jnp.float32)
            out[k] = total

        @pl.when(jnp.logical_not(owned))
        def _():
            out[k] = jnp.zeros((EIG, BLK), jnp.float32)


def gather_nodes(place, counts, starts, got):
    return pl.pallas_call(
        gather_kernel,
        out_shape=sds((N_X, EIG, BLK), jnp.float32),
        in_specs=[SMEM, SMEM, SMEM, VMEM],
        out_specs=VMEM,
        name="gather_nodes",
    )(place, counts, starts, got)


def finish_kernel(place, counts, starts, got, out):
    x, z = place[0], place[1]
    start = starts[x]
    owned = counts[x * N_Z + z]
    scale = 1.0 / (SEQ_LEN * SEQ_LEN * SEQS)
    for s in range(CAP):
        plane = lax.rem(start + s, N_X)

        @pl.when(s < owned)
        def _():
            out[0, s] = got[plane].T * scale

        @pl.when(s >= owned)
        def _():
            out[0, s] = jnp.zeros((BLK, EIG), jnp.float32)


def finish(place, counts, starts, got):
    return pl.pallas_call(
        finish_kernel,
        out_shape=sds((1, CAP, BLK, EIG), jnp.float32),
        in_specs=[SMEM, SMEM, SMEM, VMEM],
        out_specs=VMEM,
        name="finish",
    )(place, counts, starts, got)


def index(y, core, x, z):
    return ((2 * y + core) * N_X + x) * N_Z + z


def ring(core, place):
    return (place - 2 * core) % N_Z


def group_exchange(v):
    groups = [
        [index(y, c, x, ring(c, start + near + far)) for x in range(N_X) for far in (0, 2)]
        for y in range(4)
        for c in range(2)
        for start in range(0, N_Z, 4)
        for near in range(2)
    ]
    return lax.all_to_all(v, SECTION + DP, 0, 0, axis_index_groups=groups, tiled=True)


def swap(v, first):
    pairs = [(first + p, first + p + 1) for p in range(0, N_Z, 2)]
    pairs += [(b, a) for a, b in pairs]
    return lax.ppermute(v, "z", [(a % N_Z, b % N_Z) for a, b in pairs])


def shift(v, axis, k):
    n = lax.axis_size(axis)
    return v if k == 0 else lax.ppermute(v, axis, [(i, (i + k) % n) for i in range(n)])


def chip_sums(update):
    core = lax.axis_index("c")
    own = update[0].reshape(TOK, D)
    mine = lax.dynamic_slice_in_dim(own, core * (D // 2), D // 2, 1)
    theirs = shift(lax.dynamic_slice_in_dim(own, (1 - core) * (D // 2), D // 2, 1), "c", 1)
    pair = (mine.astype(jnp.float32) + theirs.astype(jnp.float32)).astype(jnp.bfloat16)
    return mine, theirs, pair, lax.ppermute(pair, "y", [(0, 1), (1, 2), (2, 3)])


def stream(mine, theirs, pair, one):
    core = lax.axis_index("c")
    mine, theirs = mine.astype(jnp.float32), theirs.astype(jnp.float32)
    two = (pair.astype(jnp.float32) + one.astype(jnp.float32)).astype(jnp.bfloat16)
    before = one.astype(jnp.float32) + lax.ppermute(two, "y", [(0, 2), (1, 3)]).astype(jnp.float32)
    low = before + jnp.where(core == 0, mine, theirs)
    high = low + jnp.where(core == 0, theirs, mine)
    low, high = low.astype(jnp.bfloat16), high.astype(jnp.bfloat16)
    return jnp.where(core == 0, low, high), shift(jnp.where(core == 0, high, low), "c", 1)


def per_device(update, outgrad, basis, counts):
    x, z, core = lax.axis_index("x"), lax.axis_index("z"), lax.axis_index("c")
    place = jnp.stack([x, z, core, (z + 2 * core) % 4]).astype(jnp.int32)
    line = lax.all_to_all(jnp.broadcast_to(basis, (N_Z,) + basis.shape[1:]), "z", 0, 0, tiled=True)
    line = line.reshape(PLANE, EIG)
    kept, up, down, column_of, starts = deal(place, counts, outgrad)
    mine, theirs, pair, one = chip_sums(update)
    grads = [kept, swap(up, 0), swap(down, 1)]
    bases = [shift(line, "x", dx) for dx in range(N_X)]
    mine, other = stream(mine, theirs, pair, one)
    rotated = rotate(place, mine, other, bases)
    rotated, grads = lax.optimization_barrier((rotated, grads))
    got = group_exchange(square([rotated, swap(rotated, 0), swap(rotated, 1)], grads))
    got = lax.all_to_all(group_sums(place, column_of, got), "z", 0, 0, tiled=True)
    got = lax.all_to_all(gather_nodes(place, counts, starts, got), "x", 0, 0, tiled=True)
    return finish(place, counts, starts, got)


def solution(mesh):
    fine = Mesh(mesh.devices.reshape(4, 2, N_X, N_Z), SECTION + DP)
    return jax.shard_map(
        per_device,
        mesh=fine,
        in_specs=(P(SECTION, DP, None, None), P(SECTION, DP, None, None), P(SECTION, DP, None), P()),
        out_specs=P(SECTION, DP, None, None),
        check_vma=False,
    )
```

```python
import jax
import jax.numpy as jnp
from jax import lax
from jax.experimental import pallas as pl
from jax.experimental.pallas import tpu as pltpu
from jax.sharding import Mesh
from jax.sharding import PartitionSpec as P

D = 5120
FW = 13824
BLK = 128
EIG = 128
SEQ_LEN = 64
SEQS = 128
NBLK = FW // BLK
CAP = 4
N_X = 4
N_Z = 16
TOK = 128
PLANE = D // N_X
SLOTS = 56
WID = SLOTS * BLK
PER = 7
GROUP = 8
SECTION = ("y", "c")
DP = ("x", "z")

SMEM = pl.BlockSpec(memory_space=pltpu.SMEM)
VMEM = pl.BlockSpec(memory_space=pltpu.VMEM)


def sds(shape, dtype):
    return jax.ShapeDtypeStruct(shape, dtype)


def mod(a, n):
    return lax.rem(a + 4 * n, n)


def rotate_kernel(place, mine, other, *refs):
    bases = refs[:N_X]
    out, full = refs[N_X:]
    x, core = place[0], place[2]
    full[core] = mine[...]
    full[1 - core] = other[...]
    total = jnp.zeros((TOK, EIG), jnp.float32)
    for dx in range(N_X):
        rows = mod(x - dx, N_X)
        lane = pl.multiple_of(lax.rem(rows, 2) * PLANE, 128)
        part = full[rows // 2, :, pl.ds(lane, PLANE)]
        total = total + jnp.dot(part, bases[dx][...], preferred_element_type=jnp.float32)
    out[...] = total.T.astype(jnp.bfloat16)


def rotate(place, mine, other, bases):
    return pl.pallas_call(
        rotate_kernel,
        out_shape=sds((EIG, TOK), jnp.bfloat16),
        in_specs=[SMEM] + [VMEM] * (2 + N_X),
        out_specs=VMEM,
        scratch_shapes=[pltpu.VMEM((2, TOK, D // 2), jnp.bfloat16)],
        compiler_params=pltpu.CompilerParams(vmem_limit_bytes=32 * 2**20),
        name="rotate",
    )(place, mine, other, *bases)


def deal_kernel(place, counts, outgrad, kept, sent, column_of, starts, offsets, block_of):
    z = place[1]

    def prefix(o, run):
        offsets[o] = run
        return run + counts[o]

    lax.fori_loop(0, N_X * N_Z, prefix, jnp.int32(0), unroll=8)

    def owner(i, g):
        column = i // N_X
        o = lax.rem(i, N_X) * N_Z + column

        @pl.when(column == z)
        def _():
            starts[lax.rem(i, N_X)] = g

        for s in range(CAP):
            block_of[g + s] = jnp.minimum(offsets[o] + s, NBLK - 1)
            column_of[g + s] = column
        return g + counts[o]

    lax.fori_loop(0, N_X * N_Z, owner, jnp.int32(0), unroll=4)
    for g in range(NBLK, 128):
        column_of[g] = N_Z
        block_of[g] = 0
    for m, out in enumerate((kept, sent)):
        near = lax.rem(place[3] + m, 2)
        for i in range(SLOTS):
            g = 16 * (i // 8) + 8 * (i // 4 % 2) + 4 * near + i % 4
            lane = pl.multiple_of(block_of[g] * BLK, BLK)
            for n in range(2):
                rows = slice(n * SEQ_LEN, (n + 1) * SEQ_LEN)
                out[rows, i * BLK : (i + 1) * BLK] = outgrad[0, n, :, pl.ds(lane, BLK)]


def deal(place, counts, outgrad):
    return pl.pallas_call(
        deal_kernel,
        out_shape=[sds((TOK, WID), jnp.bfloat16)] * 2 + [sds((128,), jnp.int32), sds((N_X,), jnp.int32)],
        in_specs=[SMEM, SMEM, VMEM],
        out_specs=[VMEM, VMEM, SMEM, SMEM],
        scratch_shapes=[pltpu.SMEM((N_X * N_Z,), jnp.int32), pltpu.SMEM((128,), jnp.int32)],
        compiler_params=pltpu.CompilerParams(vmem_limit_bytes=32 * 2**20),
        name="deal_blocks",
    )(place, counts, outgrad)


def square_kernel(*refs):
    rots, grads = refs[:2], refs[2:4]
    out, lhs = refs[4:]
    lane = lax.broadcasted_iota(jnp.int32, (EIG, TOK), 1)
    zero = jnp.zeros((EIG, TOK), jnp.bfloat16)
    for m in range(2):
        lhs[m, :EIG, :] = jnp.where(lane < SEQ_LEN, rots[m][...], zero)
        lhs[m, EIG:, :] = jnp.where(lane < SEQ_LEN, zero, rots[m][...])
    for i in range(0, SLOTS, 2):
        total = None
        for m in range(2):
            made = jnp.dot(lhs[m], grads[m][:, i * BLK : (i + 2) * BLK], preferred_element_type=jnp.float32)
            made = made * made
            made = made[:EIG] + made[EIG:]
            total = made if m == 0 else total + made
        for k in range(2):
            member = 2 * ((i + k) % 4) + (i + k) // 4 % 2
            out[member, i // 8] = total[:, k * BLK : (k + 1) * BLK].astype(out.dtype)


def square(rots, grads):
    return pl.pallas_call(
        square_kernel,
        out_shape=sds((GROUP, PER, EIG, BLK), jnp.bfloat16),
        in_specs=[VMEM] * 4,
        out_specs=VMEM,
        scratch_shapes=[pltpu.VMEM((2, 2 * EIG, TOK), jnp.bfloat16)],
        compiler_params=pltpu.CompilerParams(vmem_limit_bytes=32 * 2**20),
        name="square_sums",
    )(*rots, *grads)


def group_kernel(place, column_of, got, out):
    first = 4 * place[3] + place[0]
    out[...] = jnp.zeros(out.shape, out.dtype)
    for j in range(PER):
        column = column_of[16 * j + first]

        @pl.when(column < N_Z)
        def _():
            total = got[0, j].astype(jnp.float32)
            for r in range(1, GROUP):
                total = total + got[r, j].astype(jnp.float32)
            out[column] = total.astype(out.dtype)


def group_sums(place, column_of, got):
    return pl.pallas_call(
        group_kernel,
        out_shape=sds((N_Z, EIG, BLK), jnp.bfloat16),
        in_specs=[SMEM, SMEM, VMEM],
        out_specs=VMEM,
        name="group_sums",
    )(place, column_of, got)


def gather_kernel(place, counts, starts, got, out):
    x, z, core = place[0], place[1], place[2]
    for k in range(N_X):
        start = starts[k]
        g = start + mod(x - start + 128, N_X)
        member = lax.rem(g // 4 + 2 * core, 4)
        owned = g < start + counts[k * N_Z + z]

        @pl.when(owned)
        def _():
            total = got[member].astype(jnp.float32)
            for far in range(4, N_Z, 4):
                total = total + got[member + far].astype(jnp.float32)
            out[k] = total

        @pl.when(jnp.logical_not(owned))
        def _():
            out[k] = jnp.zeros((EIG, BLK), jnp.float32)


def gather_nodes(place, counts, starts, got):
    return pl.pallas_call(
        gather_kernel,
        out_shape=sds((N_X, EIG, BLK), jnp.float32),
        in_specs=[SMEM, SMEM, SMEM, VMEM],
        out_specs=VMEM,
        name="gather_nodes",
    )(place, counts, starts, got)


def finish_kernel(place, counts, starts, got, out):
    x, z = place[0], place[1]
    start = starts[x]
    owned = counts[x * N_Z + z]
    scale = 1.0 / (SEQ_LEN * SEQ_LEN * SEQS)
    for s in range(CAP):
        plane = lax.rem(start + s, N_X)

        @pl.when(s < owned)
        def _():
            out[0, s] = got[plane].T * scale

        @pl.when(s >= owned)
        def _():
            out[0, s] = jnp.zeros((BLK, EIG), jnp.float32)


def finish(place, counts, starts, got):
    return pl.pallas_call(
        finish_kernel,
        out_shape=sds((1, CAP, BLK, EIG), jnp.float32),
        in_specs=[SMEM, SMEM, SMEM, VMEM],
        out_specs=VMEM,
        name="finish",
    )(place, counts, starts, got)


def index(y, core, x, z):
    return ((2 * y + core) * N_X + x) * N_Z + z


def ring(core, place):
    return (place - 2 * core) % N_Z


def group_exchange(v):
    groups = [
        [index(y, c, x, ring(c, start + near + far)) for x in range(N_X) for far in (0, 2)]
        for y in range(4)
        for c in range(2)
        for start in range(0, N_Z, 4)
        for near in range(2)
    ]
    return lax.all_to_all(v, SECTION + DP, 0, 0, axis_index_groups=groups, tiled=True)


def pass_on(v):
    perm = [(c * N_Z + z, c * N_Z + (z + 1 - 2 * c) % N_Z) for c in range(2) for z in range(N_Z)]
    return lax.ppermute(v, ("c", "z"), perm)


def shift(v, axis, k):
    n = lax.axis_size(axis)
    return v if k == 0 else lax.ppermute(v, axis, [(i, (i + k) % n) for i in range(n)])


def chip_sums(update):
    core = lax.axis_index("c")
    own = update[0].reshape(TOK, D)
    mine = lax.dynamic_slice_in_dim(own, core * (D // 2), D // 2, 1)
    theirs = shift(lax.dynamic_slice_in_dim(own, (1 - core) * (D // 2), D // 2, 1), "c", 1)
    pair = (mine.astype(jnp.float32) + theirs.astype(jnp.float32)).astype(jnp.bfloat16)
    return mine, theirs, pair, lax.ppermute(pair, "y", [(0, 1), (1, 2), (2, 3)])


def stream(mine, theirs, pair, one):
    core = lax.axis_index("c")
    mine, theirs = mine.astype(jnp.float32), theirs.astype(jnp.float32)
    two = (pair.astype(jnp.float32) + one.astype(jnp.float32)).astype(jnp.bfloat16)
    before = one.astype(jnp.float32) + lax.ppermute(two, "y", [(0, 2), (1, 3)]).astype(jnp.float32)
    low = before + jnp.where(core == 0, mine, theirs)
    high = low + jnp.where(core == 0, theirs, mine)
    low, high = low.astype(jnp.bfloat16), high.astype(jnp.bfloat16)
    return jnp.where(core == 0, low, high), shift(jnp.where(core == 0, high, low), "c", 1)


def per_device(update, outgrad, basis, counts):
    x, z, core = lax.axis_index("x"), lax.axis_index("z"), lax.axis_index("c")
    place = jnp.stack([x, z, core, (z + 2 * core) % 4]).astype(jnp.int32)
    line = lax.all_to_all(jnp.broadcast_to(basis, (N_Z,) + basis.shape[1:]), "z", 0, 0, tiled=True)
    line = line.reshape(PLANE, EIG)
    kept, sent, column_of, starts = deal(place, counts, outgrad)
    mine, theirs, pair, one = chip_sums(update)
    grads = [kept, pass_on(sent)]
    bases = [shift(line, "x", dx) for dx in range(N_X)]
    mine, other = stream(mine, theirs, pair, one)
    rotated = rotate(place, mine, other, bases)
    rotated, grads = lax.optimization_barrier((rotated, grads))
    got = group_exchange(square([rotated, pass_on(rotated)], grads))
    got = lax.all_to_all(group_sums(place, column_of, got), "z", 0, 0, tiled=True)
    got = lax.all_to_all(gather_nodes(place, counts, starts, got), "x", 0, 0, tiled=True)
    return finish(place, counts, starts, got)


def solution(mesh):
    fine = Mesh(mesh.devices.reshape(4, 2, N_X, N_Z), SECTION + DP)
    return jax.shard_map(
        per_device,
        mesh=fine,
        in_specs=(P(SECTION, DP, None, None), P(SECTION, DP, None, None), P(SECTION, DP, None), P()),
        out_specs=P(SECTION, DP, None, None),
        check_vma=False,
    )
```

```python
import jax
import jax.numpy as jnp
from jax import lax
from jax.experimental import pallas as pl
from jax.experimental.pallas import tpu as pltpu
from jax.sharding import Mesh
from jax.sharding import PartitionSpec as P

D = 5120
FW = 13824
BLK = 128
EIG = 128
SEQ_LEN = 64
SEQS = 128
NBLK = FW // BLK
CAP = 4
N_X = 4
N_Z = 16
TOK = 128
PLANE = D // N_X
SLOTS = 56
WID = SLOTS * BLK
PER = 7
GROUP = 8
SECTION = ("y", "c")
DP = ("x", "z")

SMEM = pl.BlockSpec(memory_space=pltpu.SMEM)
VMEM = pl.BlockSpec(memory_space=pltpu.VMEM)


def sds(shape, dtype):
    return jax.ShapeDtypeStruct(shape, dtype)


def mod(a, n):
    return lax.rem(a + 4 * n, n)


def rotate_kernel(place, mine, other, *refs):
    bases = refs[:N_X]
    out, full = refs[N_X:]
    x, core = place[0], place[2]
    full[core] = mine[...]
    full[1 - core] = other[...]
    total = jnp.zeros((TOK, EIG), jnp.float32)
    for dx in range(N_X):
        rows = mod(x - dx, N_X)
        lane = pl.multiple_of(lax.rem(rows, 2) * PLANE, 128)
        part = full[rows // 2, :, pl.ds(lane, PLANE)]
        total = total + jnp.dot(part, bases[dx][...], preferred_element_type=jnp.float32)
    out[...] = total.T.astype(jnp.bfloat16)


def rotate(place, mine, other, bases):
    return pl.pallas_call(
        rotate_kernel,
        out_shape=sds((EIG, TOK), jnp.bfloat16),
        in_specs=[SMEM] + [VMEM] * (2 + N_X),
        out_specs=VMEM,
        scratch_shapes=[pltpu.VMEM((2, TOK, D // 2), jnp.bfloat16)],
        compiler_params=pltpu.CompilerParams(vmem_limit_bytes=32 * 2**20),
        name="rotate",
    )(place, mine, other, *bases)


def deal_kernel(place, counts, outgrad, kept, sent, column_of, offsets, block_of):
    z = place[1]

    def prefix(o, run):
        offsets[o] = run
        return run + counts[o]

    lax.fori_loop(0, N_X * N_Z, prefix, jnp.int32(0), unroll=8)

    def owner(i, g):
        column = i // N_X
        o = lax.rem(i, N_X) * N_Z + column

        @pl.when(column == z)
        def _():
            column_of[128 + lax.rem(i, N_X)] = g

        for s in range(CAP):
            block_of[g + s] = jnp.minimum(offsets[o] + s, NBLK - 1)
            column_of[g + s] = column
        return g + counts[o]

    lax.fori_loop(0, N_X * N_Z, owner, jnp.int32(0), unroll=4)
    for g in range(NBLK, 128):
        column_of[g] = N_Z
        block_of[g] = 0
    for m, out in enumerate((kept, sent)):
        near = lax.rem(place[3] + m, 2)
        for i in range(SLOTS):
            g = 16 * (i // 8) + 8 * (i // 4 % 2) + 4 * near + i % 4
            lane = pl.multiple_of(block_of[g] * BLK, BLK)
            for n in range(2):
                rows = slice(n * SEQ_LEN, (n + 1) * SEQ_LEN)
                out[rows, i * BLK : (i + 1) * BLK] = outgrad[0, n, :, pl.ds(lane, BLK)]


def deal(place, counts, outgrad):
    return pl.pallas_call(
        deal_kernel,
        out_shape=[sds((TOK, WID), jnp.bfloat16)] * 2 + [sds((256,), jnp.int32)],
        in_specs=[SMEM, SMEM, VMEM],
        out_specs=[VMEM, VMEM, SMEM],
        scratch_shapes=[pltpu.SMEM((N_X * N_Z,), jnp.int32), pltpu.SMEM((128,), jnp.int32)],
        compiler_params=pltpu.CompilerParams(vmem_limit_bytes=32 * 2**20),
        name="deal_blocks",
    )(place, counts, outgrad)


def square_kernel(*refs):
    rots, grads = refs[:2], refs[2:4]
    out, lhs = refs[4:]
    lane = lax.broadcasted_iota(jnp.int32, (EIG, TOK), 1)
    zero = jnp.zeros((EIG, TOK), jnp.bfloat16)
    for m in range(2):
        lhs[m, :EIG, :] = jnp.where(lane < SEQ_LEN, rots[m][...], zero)
        lhs[m, EIG:, :] = jnp.where(lane < SEQ_LEN, zero, rots[m][...])
    for i in range(0, SLOTS, 2):
        total = None
        for m in range(2):
            made = jnp.dot(lhs[m], grads[m][:, i * BLK : (i + 2) * BLK], preferred_element_type=jnp.float32)
            made = made * made
            made = made[:EIG] + made[EIG:]
            total = made if m == 0 else total + made
        for k in range(2):
            member = 2 * ((i + k) % 4) + (i + k) // 4 % 2
            out[member, i // 8] = total[:, k * BLK : (k + 1) * BLK].astype(out.dtype)


def square(rots, grads):
    return pl.pallas_call(
        square_kernel,
        out_shape=sds((GROUP, PER, EIG, BLK), jnp.bfloat16),
        in_specs=[VMEM] * 4,
        out_specs=VMEM,
        scratch_shapes=[pltpu.VMEM((2, 2 * EIG, TOK), jnp.bfloat16)],
        compiler_params=pltpu.CompilerParams(vmem_limit_bytes=32 * 2**20),
        name="square_sums",
    )(*rots, *grads)


def group_kernel(place, column_of, got, out):
    first = 4 * place[3] + place[0]
    for j in range(PER):
        column = column_of[16 * j + first]

        @pl.when(column < N_Z)
        def _():
            total = got[0, j].astype(jnp.float32)
            for r in range(1, GROUP):
                total = total + got[r, j].astype(jnp.float32)
            out[column] = total.astype(out.dtype)


def group_sums(place, column_of, got):
    return pl.pallas_call(
        group_kernel,
        out_shape=sds((N_Z, EIG, BLK), jnp.bfloat16),
        in_specs=[SMEM, SMEM, VMEM],
        out_specs=VMEM,
        name="group_sums",
    )(place, column_of, got)


def gather_kernel(place, counts, starts, got, out):
    x, z, core = place[0], place[1], place[2]
    for k in range(N_X):
        start = starts[128 + k]
        g = start + mod(x - start + 128, N_X)
        member = lax.rem(g // 4 + 2 * core, 4)
        owned = g < start + counts[k * N_Z + z]

        @pl.when(owned)
        def _():
            total = got[member].astype(jnp.float32)
            for far in range(4, N_Z, 4):
                total = total + got[member + far].astype(jnp.float32)
            out[k] = total

        @pl.when(jnp.logical_not(owned))
        def _():
            out[k] = jnp.zeros((EIG, BLK), jnp.float32)


def gather_nodes(place, counts, starts, got):
    return pl.pallas_call(
        gather_kernel,
        out_shape=sds((N_X, EIG, BLK), jnp.float32),
        in_specs=[SMEM, SMEM, SMEM, VMEM],
        out_specs=VMEM,
        name="gather_nodes",
    )(place, counts, starts, got)


def finish_kernel(place, counts, starts, got, out):
    x, z = place[0], place[1]
    start = starts[128 + x]
    owned = counts[x * N_Z + z]
    scale = 1.0 / (SEQ_LEN * SEQ_LEN * SEQS)
    for s in range(CAP):
        plane = lax.rem(start + s, N_X)

        @pl.when(s < owned)
        def _():
            out[0, s] = got[plane].T * scale

        @pl.when(s >= owned)
        def _():
            out[0, s] = jnp.zeros((BLK, EIG), jnp.float32)


def finish(place, counts, starts, got):
    return pl.pallas_call(
        finish_kernel,
        out_shape=sds((1, CAP, BLK, EIG), jnp.float32),
        in_specs=[SMEM, SMEM, SMEM, VMEM],
        out_specs=VMEM,
        name="finish",
    )(place, counts, starts, got)


def index(y, core, x, z):
    return ((2 * y + core) * N_X + x) * N_Z + z


def ring(core, place):
    return (place - 2 * core) % N_Z


def group_exchange(v):
    groups = [
        [index(y, c, x, ring(c, start + near + far)) for x in range(N_X) for far in (0, 2)]
        for y in range(4)
        for c in range(2)
        for start in range(0, N_Z, 4)
        for near in range(2)
    ]
    return lax.all_to_all(v, SECTION + DP, 0, 0, axis_index_groups=groups, tiled=True)


def pass_on(v):
    perm = [(c * N_Z + z, c * N_Z + (z + 1 - 2 * c) % N_Z) for c in range(2) for z in range(N_Z)]
    return lax.ppermute(v, ("c", "z"), perm)


def shift(v, axis, k):
    n = lax.axis_size(axis)
    return v if k == 0 else lax.ppermute(v, axis, [(i, (i + k) % n) for i in range(n)])


def chip_sums(update):
    core = lax.axis_index("c")
    own = update[0].reshape(TOK, D)
    mine = lax.dynamic_slice_in_dim(own, core * (D // 2), D // 2, 1)
    theirs = shift(lax.dynamic_slice_in_dim(own, (1 - core) * (D // 2), D // 2, 1), "c", 1)
    return mine, theirs, (mine.astype(jnp.float32) + theirs.astype(jnp.float32)).astype(jnp.bfloat16)


def stream(mine, theirs, pair):
    core = lax.axis_index("c")
    mine, theirs = mine.astype(jnp.float32), theirs.astype(jnp.float32)
    steps = [lax.ppermute(pair, "y", [(i, i + k) for i in range(4 - k)]) for k in range(1, 4)]
    before = steps[0].astype(jnp.float32) + steps[1].astype(jnp.float32) + steps[2].astype(jnp.float32)
    low = before + jnp.where(core == 0, mine, theirs)
    high = low + jnp.where(core == 0, theirs, mine)
    low, high = low.astype(jnp.bfloat16), high.astype(jnp.bfloat16)
    return jnp.where(core == 0, low, high), shift(jnp.where(core == 0, high, low), "c", 1)


def per_device(update, outgrad, basis, counts):
    x, z, core = lax.axis_index("x"), lax.axis_index("z"), lax.axis_index("c")
    place = jnp.stack([x, z, core, (z + 2 * core) % 4]).astype(jnp.int32)
    line = lax.all_to_all(jnp.broadcast_to(basis, (N_Z,) + basis.shape[1:]), "z", 0, 0, tiled=True)
    line = line.reshape(PLANE, EIG)
    kept, sent, table = deal(place, counts, outgrad)
    mine, theirs, pair = chip_sums(update)
    grads = [kept, pass_on(sent)]
    bases = [shift(line, "x", dx) for dx in range(N_X)]
    mine, other = stream(mine, theirs, pair)
    rotated = rotate(place, mine, other, bases)
    rotated, grads = lax.optimization_barrier((rotated, grads))
    got = group_exchange(square([rotated, pass_on(rotated)], grads))
    got = lax.all_to_all(group_sums(place, table, got), "z", 0, 0, tiled=True)
    got = lax.all_to_all(gather_nodes(place, counts, table, got), "x", 0, 0, tiled=True)
    return finish(place, counts, table, got)


def solution(mesh):
    fine = Mesh(mesh.devices.reshape(4, 2, N_X, N_Z), SECTION + DP)
    return jax.shard_map(
        per_device,
        mesh=fine,
        in_specs=(P(SECTION, DP, None, None), P(SECTION, DP, None, None), P(SECTION, DP, None), P()),
        out_specs=P(SECTION, DP, None, None),
        check_vma=False,
    )
```
